32 devices in a mesh: grp: 2 (over x), blk: 16 (over z, y, core).
Axes of the slice: x: 2, y: 2, z: 4, core: 2. Of those that a mesh axis runs over, the one named last changes fastest.
Arguments:
- observed: bfloat16 [512, 16384], P(('grp', 'blk')), parts along dimension 0, may hold values from 0.03 to 2.1, as said below
- good_pixel_mask: int32 [512, 16384], P(('grp', 'blk')), parts along dimension 0, may hold values from 0 to 1, as said below
- templates: bfloat16 [512, 65632], P(('grp', 'blk')), parts along dimension 0, may hold values from -6 to 6
- template_kernel_index: int32 [512], P(('grp', 'blk')), parts along dimension 0, may hold values from 0 to 7
- line_spread_table: float32 [8, 97], replicated, may hold values from 0.05 to 1
- exposure_per_row: int32 [512], P('grp'), parts along dimension 0, may hold values from 0 to 255, each once
Outputs:
- ccf: float32 [512, 16384], P('grp', 'blk'), parts along dimension 0
The draws below stay inside these ranges and needn't reach their ends.
There are 2 independent parts, one for each index of `grp`. The reference program is written for one: setup_inputs(seed, part) draws one part's arguments, and reference() takes and returns one part's arrays. A program takes and returns all parts, laid end to end along the dimension named above; an argument that names none is the same for every part. Nothing has to cross between parts.
Inputs may be any that keep to these rules, and one draw needn't show every extreme that they name: observed flux is positive, so masked is above zero exactly on good pixels. `good_pixel_mask`: some pixel columns are bad in every exposure.
All inputs are finite; a program needn't handle non-finite values.
Results may differ from the reference program's by a relative error of at most 0.0015.
Values may be sent and summed in bfloat16 or wider, within the bound.
A program may use at most 128 MiB of HBM per device.

```python
import math
import jax
import jax.numpy as jnp
from jax import lax

PIX = 16384
LAGS = 64
KERNEL_TAPS = 97
KERNEL_COUNT = 8
OBS = 256
NT = 256
HL = 65632


def draw_observed(key, part):
    key_base, key_gain, key_noise = jax.random.split(jax.random.fold_in(key, 11), 3)
    rows = jnp.arange(OBS, dtype=jnp.float32) / OBS
    gain = (0.5 + rows) * jax.random.uniform(key_gain, (OBS,), jnp.float32, 0.8, 1.2)
    base = jnp.exp(jax.random.uniform(key_base, (PIX,), jnp.float32, -2.302585, 0.0))
    noise = jax.random.uniform(key_noise, (OBS, PIX), jnp.float32, -0.15, 0.15)
    flux = base[None, :] * gain[:, None] * (1.0 + noise)
    return flux.astype(jnp.bfloat16)


def draw_good_pixel_mask(key, part):
    key_cols, key_hits = jax.random.split(jax.random.fold_in(key, 23))
    good_cols = jax.random.randint(key_cols, (PIX,), 0, 16) != 0
    good_hits = jax.random.randint(key_hits, (OBS, PIX), 0, 10) != 0
    return (good_cols[None, :] & good_hits).astype(jnp.int32)


def touch_ends(array, stream_key, low, high):
    longest = array.shape.index(max(array.shape))
    spots = []
    for shift in (0, 1):
        where = [jax.random.randint(jax.random.fold_in(stream_key, axis), (), 0, length) for axis, length in enumerate(array.shape)]
        where[longest] = (where[longest] + shift) % array.shape[longest]
        spots.append(tuple(where))
    return array.at[spots[0]].set(low).at[spots[1]].set(high)


def level_of(rng, extent, shards, smallest, high):
    loudness = 1.0
    for position, blocks in shards:
        heights = jax.random.uniform(jax.random.fold_in(jax.random.fold_in(rng, 6), position), (blocks,), jnp.float32, smallest / len(shards), high / len(shards))
        loudness = loudness * jnp.repeat(jnp.exp(heights), extent[position] // blocks).reshape((-1,) + (1,) * (len(extent) - 1 - position))
    return loudness


def normal_values(own_key, extent, deviation, bound, cuts=(), kind=jnp.bfloat16):
    result = jax.random.normal(own_key, extent, jnp.float32) * deviation
    if len(cuts) > 0:
        result = level_of(own_key, extent, cuts, -0.22, 0.18) * result
    return jnp.clip(result, min=-bound, max=bound).astype(kind)


def setup_inputs(seed: int = 0, part: int = 0) -> dict:
    keys = jax.random.split(jax.random.key(seed), 7)
    own_keys = jax.random.split(jax.random.fold_in(keys[6], part), 7)
    observed = draw_observed(jax.random.fold_in(jax.random.fold_in(keys[6], part), 71), part)
    good_pixel_mask = draw_good_pixel_mask(jax.random.fold_in(jax.random.fold_in(keys[6], part), 71), part)
    templates = normal_values(own_keys[2], (NT, HL), 1.0, 6.0, ((0, 16),))
    template_kernel_index = touch_ends(jax.random.randint(own_keys[3], (NT,), 0, KERNEL_COUNT), jax.random.fold_in(own_keys[3], 1), 0, KERNEL_COUNT - 1).astype(jnp.int32)
    line_spread_table = jnp.clip(jnp.exp(jax.random.uniform(keys[4], (KERNEL_COUNT, KERNEL_TAPS), jnp.float32, math.log(0.05), math.log(1.0))), 0.05, 1.0)
    exposure_per_row = jax.random.permutation(own_keys[5], OBS).astype(jnp.int32)
    return {"observed": observed, "good_pixel_mask": good_pixel_mask, "templates": templates, "template_kernel_index": template_kernel_index, "line_spread_table": line_spread_table, "exposure_per_row": exposure_per_row}


def broadened_templates(templates, template_kernel_index, line_spread_table):
    count_t = templates.shape[0]
    kernel_selector = (template_kernel_index[:, None] == jnp.arange(KERNEL_COUNT, dtype=jnp.int32)[None, :]).astype(jnp.float32)
    kernel_weights = jnp.dot(kernel_selector, line_spread_table, precision=lax.Precision.HIGHEST, preferred_element_type=jnp.float32)
    q_count = (KERNEL_TAPS + 3) // 4
    kernel_weights = jnp.pad(kernel_weights, ((0, 0), (0, 4 * q_count - KERNEL_TAPS))).reshape(count_t, q_count, 4)
    phases = templates.reshape(count_t, PIX + 24, 4).transpose(0, 2, 1)
    smoothed_flux = jnp.zeros((count_t, PIX), jnp.float32)
    for q in range(q_count):
        window = phases[:, :, q:q + PIX].astype(jnp.float32)
        smoothed_flux = smoothed_flux + lax.optimization_barrier(jnp.sum(kernel_weights[:, q, :, None] * window, axis=1))
    return smoothed_flux

def reference(observed, good_pixel_mask, templates, template_kernel_index, line_spread_table, exposure_per_row):
    masked = observed * (good_pixel_mask > 0).astype(jnp.bfloat16)
    present = (masked > 0).astype(jnp.float32)
    flux = masked.astype(jnp.float32)
    count = lax.optimization_barrier(jnp.sum(present, axis=0))
    mean = lax.optimization_barrier(jnp.sum(flux, axis=0)) / jnp.maximum(count, 1.0)
    resid = present * (flux - mean[None, :])
    scale = lax.rsqrt(lax.optimization_barrier(jnp.sum(resid * resid, axis=1)) / PIX + 1e-06)
    ready = (resid * scale[:, None]).astype(jnp.bfloat16).astype(jnp.float32)
    smoothed_flux = broadened_templates(templates, template_kernel_index, line_spread_table)
    shaped = (smoothed_flux * lax.rsqrt(lax.optimization_barrier(jnp.sum(smoothed_flux * smoothed_flux, axis=1, keepdims=True)) / PIX + 1e-06)).astype(jnp.bfloat16)
    padded = jnp.pad(shaped, ((0, 0), (LAGS // 2, LAGS // 2)))
    group = math.gcd(NT, 8)
    grouped = padded.reshape(NT // group, group, PIX + LAGS)

    def one_group(panel):
        band = jnp.stack([panel[:, l:l + PIX] for l in range(LAGS)], axis=2).astype(jnp.float32)
        return jnp.einsum('oj,tjl->otl', ready, band)
    cross = lax.map(one_group, grouped)
    cross = cross.transpose(1, 0, 2, 3).reshape(OBS, NT * LAGS) / jnp.float32(math.sqrt(PIX))
    return jnp.zeros_like(cross).at[exposure_per_row].set(cross)
```

```python
import functools
import math

import jax
import jax.numpy as jnp
from jax import lax
from jax.experimental import pallas as pl
from jax.experimental.pallas import tpu as pltpu
from jax.sharding import PartitionSpec as P

PIX = 16384
LAGS = 64
TAPS = 97
KERNELS = 8
Q = 128
R = PIX // Q
BAND = 640
F32 = jnp.float32
BF16 = jnp.bfloat16
NT_DIMS = (((1,), (1,)), ((), ()))


def template_kernel(index_ref, table_ref, templates_ref, x_ref, bands, chunks, smooth):
    count = templates_ref.shape[0]
    for k in range(KERNELS):
        row = jnp.broadcast_to(table_ref[k : k + 1, :], (Q, BAND))
        band = pltpu.roll(row, 0, 1, stride=4, stride_axis=0)
        high = band.astype(BF16)
        bands[k, :, :BAND] = high
        bands[k, :, BAND:] = (band - high.astype(F32)).astype(BF16)

    def spread(r, _):
        at = pl.multiple_of(r * (4 * Q), 128)
        piece = templates_ref[:, pl.ds(at, BAND)].astype(F32)
        for i in range(BAND // 128):
            chunks[i, pl.ds(pl.multiple_of(r * count, count), count), :] = piece[
                :, 128 * i : 128 * (i + 1)
            ]
        return 0

    lax.fori_loop(0, R - 1, spread, 0, unroll=8)
    last = (R - 1) * 4 * Q
    left = templates_ref.shape[1] - last
    tail = templates_ref[:, last:].astype(F32)
    tail = jnp.concatenate([tail, jnp.zeros((count, BAND - left), F32)], axis=1)
    for i in range(BAND // 128):
        chunks[i, (R - 1) * count :, :] = tail[:, 128 * i : 128 * (i + 1)]

    for t in range(count):
        rows = [
            chunks[i, pl.ds(t, R, stride=count), :].astype(BF16) for i in range(BAND // 128)
        ]
        rows = jnp.concatenate(rows + rows, axis=1)
        flux = lax.dot_general(
            bands[index_ref[t]], rows, NT_DIMS, preferred_element_type=F32
        )
        total = jnp.sum(flux * flux)
        smooth[pl.ds(t, Q, stride=count), :] = flux * lax.rsqrt(
            jnp.full((1, 1), total) / PIX + 1e-06
        )

    half = LAGS // 2
    body = smooth[...]
    lane = lax.broadcasted_iota(jnp.int32, (half * count, R), 1)
    x_ref[half * count : (half + Q) * count, :] = body.astype(BF16)
    before = pltpu.roll(body[(Q - half) * count :, :], 1, 1)
    x_ref[: half * count, :] = jnp.where(lane == 0, 0.0, before).astype(BF16)
    after = pltpu.roll(body[: half * count, :], R - 1, 1)
    x_ref[(half + Q) * count :, :] = jnp.where(lane == R - 1, 0.0, after).astype(BF16)


def shape_templates(templates, template_kernel_index, line_spread_table):
    count = templates.shape[0]
    table = jnp.pad(line_spread_table, ((0, 0), (0, BAND - TAPS)))
    return pl.pallas_call(
        template_kernel,
        out_shape=jax.ShapeDtypeStruct(((Q + LAGS) * count, R), BF16),
        in_specs=[
            pl.BlockSpec(memory_space=pltpu.SMEM),
            pl.BlockSpec(memory_space=pltpu.VMEM),
            pl.BlockSpec(memory_space=pltpu.VMEM),
        ],
        out_specs=pl.BlockSpec(memory_space=pltpu.VMEM),
        scratch_shapes=[
            pltpu.VMEM((KERNELS, Q, 2 * BAND), BF16),
            pltpu.VMEM((BAND // 128, R * count, 128), F32),
            pltpu.VMEM((Q * count, R), F32),
        ],
        compiler_params=pltpu.CompilerParams(vmem_limit_bytes=40 * 2**20),
        cost_estimate=pl.CostEstimate(
            flops=2 * count * Q * R * 2 * BAND, bytes_accessed=6 * 2**20, transcendentals=0
        ),
        name="shape_templates",
    )(template_kernel_index, table, templates)


def correlate_kernel(step_q, rows_ref, x_ref, g_ref, out_ref, acc):
    step = pl.program_id(0)
    total_rows = rows_ref.shape[1]
    count = x_ref.shape[0] // (Q + LAGS)
    tile = 256

    @pl.when(step == 0)
    def _():
        acc[...] = jnp.zeros_like(acc)

    right = jnp.concatenate([g_ref[i] for i in range(step_q)], axis=1)
    for m in range(LAGS * count // tile):
        left = jnp.concatenate(
            [
                x_ref[pl.ds(pl.multiple_of((step * step_q + i) * count + m * tile, 16), tile), :]
                for i in range(step_q)
            ],
            axis=1,
        )
        part = lax.dot_general(left, right, NT_DIMS, preferred_element_type=F32)
        for h in range(total_rows // 128):
            acc[h, m * tile : (m + 1) * tile, :] += part[:, 128 * h : 128 * (h + 1)]

    @pl.when(step == pl.num_programs(0) - 1)
    def _():
        place = (
            lax.broadcasted_iota(jnp.int32, (total_rows, total_rows), 0) == rows_ref[...]
        ).astype(BF16)
        both = jnp.concatenate([place, place], axis=1)
        for t in range(0, count, 2):
            part = jnp.concatenate(
                [
                    jnp.concatenate(
                        [
                            acc[h, pl.ds(t + i, LAGS, stride=count), :]
                            for h in range(total_rows // 128)
                        ],
                        axis=1,
                    )
                    for i in range(2)
                ],
                axis=0,
            ) * F32(1.0 / math.sqrt(PIX))
            high = part.astype(BF16)
            low = (part - high.astype(F32)).astype(BF16)
            out_ref[:, t * LAGS : (t + 2) * LAGS] = lax.dot_general(
                both,
                jnp.concatenate([high, low], axis=1),
                NT_DIMS,
                preferred_element_type=F32,
            )


def correlate(x, gathered, exposure_per_row):
    total_rows = gathered.shape[1]
    count = x.shape[0] // (Q + LAGS)
    step_q = 8
    return pl.pallas_call(
        functools.partial(correlate_kernel, step_q),
        grid=(Q // step_q,),
        out_shape=jax.ShapeDtypeStruct((total_rows, count * LAGS), F32),
        in_specs=[
            pl.BlockSpec((1, total_rows), lambda s: (0, 0)),
            pl.BlockSpec(x.shape, lambda s: (0, 0)),
            pl.BlockSpec((step_q, total_rows, R), lambda s: (s, 0, 0)),
        ],
        out_specs=pl.BlockSpec((total_rows, count * LAGS), lambda s: (0, 0)),
        scratch_shapes=[pltpu.VMEM((total_rows // 128, LAGS * count, 128), F32)],
        compiler_params=pltpu.CompilerParams(vmem_limit_bytes=40 * 2**20),
        name="correlate",
    )(exposure_per_row.reshape(1, total_rows), x, gathered)


def shards(
    observed, good_pixel_mask, templates, template_kernel_index, line_spread_table, exposure_per_row
):
    rows = observed.shape[0]
    x = shape_templates(templates, template_kernel_index, line_spread_table)
    good = good_pixel_mask > 0
    flux = jnp.where(good, observed, 0).astype(F32)
    present = (flux > 0).astype(F32)
    sums = lax.psum(jnp.stack([jnp.sum(flux, axis=0), jnp.sum(present, axis=0)]), "blk")
    mean = sums[0] / jnp.maximum(sums[1], 1.0)
    resid = present * (flux - mean[None, :])
    scale = lax.rsqrt(jnp.sum(resid * resid, axis=1) / PIX + 1e-06)
    ready = (resid * scale[:, None]).astype(BF16)
    ready = ready.reshape(rows, R, Q).transpose(2, 0, 1)
    gathered = lax.all_gather(ready, "blk", axis=1, tiled=True)
    return correlate(x, gathered, exposure_per_row)


def solution(mesh):
    in_specs = (
        P(("grp", "blk"), None),
        P(("grp", "blk"), None),
        P(("grp", "blk"), None),
        P(("grp", "blk")),
        P(),
        P("grp"),
    )
    out_specs = P("grp", "blk")
    return jax.shard_map(shards, mesh=mesh, in_specs=in_specs, out_specs=out_specs, check_vma=False)
```

```python
import functools
import math

import jax
import jax.numpy as jnp
from jax import lax
from jax.experimental import pallas as pl
from jax.experimental.pallas import tpu as pltpu
from jax.sharding import PartitionSpec as P

PIX = 16384
LAGS = 64
TAPS = 97
KERNELS = 8
Q = 128
R = PIX // Q
BAND = 640
F32 = jnp.float32
BF16 = jnp.bfloat16
MESH = pl.DeviceIdType.MESH
NT_DIMS = (((1,), (1,)), ((), ()))


def template_kernel(index_ref, table_ref, templates_ref, x_ref, bands, chunks, smooth):
    count = templates_ref.shape[0]
    for k in range(KERNELS):
        row = jnp.broadcast_to(table_ref[k : k + 1, :], (Q, BAND))
        band = pltpu.roll(row, 0, 1, stride=4, stride_axis=0)
        high = band.astype(BF16)
        bands[k, :, :BAND] = high
        bands[k, :, BAND:] = (band - high.astype(F32)).astype(BF16)

    def spread(r, _):
        at = pl.multiple_of(r * (4 * Q), 128)
        piece = templates_ref[:, pl.ds(at, BAND)].astype(F32)
        for i in range(BAND // 128):
            chunks[i, pl.ds(pl.multiple_of(r * count, count), count), :] = piece[
                :, 128 * i : 128 * (i + 1)
            ]
        return 0

    lax.fori_loop(0, R - 1, spread, 0, unroll=8)
    last = (R - 1) * 4 * Q
    left = templates_ref.shape[1] - last
    tail = templates_ref[:, last:].astype(F32)
    tail = jnp.concatenate([tail, jnp.zeros((count, BAND - left), F32)], axis=1)
    for i in range(BAND // 128):
        chunks[i, (R - 1) * count :, :] = tail[:, 128 * i : 128 * (i + 1)]

    for t in range(count):
        rows = [
            chunks[i, pl.ds(t, R, stride=count), :].astype(BF16) for i in range(BAND // 128)
        ]
        rows = jnp.concatenate(rows + rows, axis=1)
        flux = lax.dot_general(
            bands[index_ref[t]], rows, NT_DIMS, preferred_element_type=F32
        )
        total = jnp.sum(flux * flux)
        smooth[pl.ds(t, Q, stride=count), :] = flux * lax.rsqrt(
            jnp.full((1, 1), total) / PIX + 1e-06
        )

    half = LAGS // 2
    body = smooth[...]
    lane = lax.broadcasted_iota(jnp.int32, (half * count, R), 1)
    x_ref[half * count : (half + Q) * count, :] = body.astype(BF16)
    before = pltpu.roll(body[(Q - half) * count :, :], 1, 1)
    x_ref[: half * count, :] = jnp.where(lane == 0, 0.0, before).astype(BF16)
    after = pltpu.roll(body[: half * count, :], R - 1, 1)
    x_ref[(half + Q) * count :, :] = jnp.where(lane == R - 1, 0.0, after).astype(BF16)


def shape_templates(templates, template_kernel_index, line_spread_table):
    count = templates.shape[0]
    table = jnp.pad(line_spread_table, ((0, 0), (0, BAND - TAPS)))
    return pl.pallas_call(
        template_kernel,
        out_shape=jax.ShapeDtypeStruct(((Q + LAGS) * count, R), BF16),
        in_specs=[
            pl.BlockSpec(memory_space=pltpu.SMEM),
            pl.BlockSpec(memory_space=pltpu.VMEM),
            pl.BlockSpec(memory_space=pltpu.VMEM),
        ],
        out_specs=pl.BlockSpec(memory_space=pltpu.VMEM),
        scratch_shapes=[
            pltpu.VMEM((KERNELS, Q, 2 * BAND), BF16),
            pltpu.VMEM((BAND // 128, R * count, 128), F32),
            pltpu.VMEM((Q * count, R), F32),
        ],
        compiler_params=pltpu.CompilerParams(vmem_limit_bytes=40 * 2**20),
        cost_estimate=pl.CostEstimate(
            flops=2 * count * Q * R * 2 * BAND, bytes_accessed=6 * 2**20, transcendentals=0
        ),
        name="shape_templates",
    )(template_kernel_index, table, templates)


def place_rows(rows_ref, acc, out_ref, count):
    total_rows = rows_ref.shape[1]
    chosen = (
        lax.broadcasted_iota(jnp.int32, (total_rows, total_rows), 0) == rows_ref[...]
    ).astype(BF16)
    both = jnp.concatenate([chosen, chosen], axis=1)
    for t in range(0, count, 2):
        part = jnp.concatenate(
            [
                jnp.concatenate(
                    [
                        acc[h, pl.ds(t + i, LAGS, stride=count), :]
                        for h in range(total_rows // 128)
                    ],
                    axis=1,
                )
                for i in range(2)
            ],
            axis=0,
        ) * F32(1.0 / math.sqrt(PIX))
        high = part.astype(BF16)
        low = (part - high.astype(F32)).astype(BF16)
        out_ref[:, t * LAGS : (t + 2) * LAGS] = lax.dot_general(
            both,
            jnp.concatenate([high, low], axis=1),
            NT_DIMS,
            preferred_element_type=F32,
        )


def correlate_kernel(step_q, rows_ref, x_ref, g_ref, out_ref, acc):
    step = pl.program_id(0)
    total_rows = rows_ref.shape[1]
    count = x_ref.shape[0] // (Q + LAGS)
    tile = 256

    @pl.when(step == 0)
    def _():
        acc[...] = jnp.zeros_like(acc)

    right = jnp.concatenate([g_ref[i] for i in range(step_q)], axis=1)
    for m in range(LAGS * count // tile):
        left = jnp.concatenate(
            [
                x_ref[pl.ds(pl.multiple_of((step * step_q + i) * count + m * tile, 16), tile), :]
                for i in range(step_q)
            ],
            axis=1,
        )
        part = lax.dot_general(left, right, NT_DIMS, preferred_element_type=F32)
        for h in range(total_rows // 128):
            acc[h, m * tile : (m + 1) * tile, :] += part[:, 128 * h : 128 * (h + 1)]

    @pl.when(step == pl.num_programs(0) - 1)
    def _():
        place_rows(rows_ref, acc, out_ref, count)


def correlate(x, gathered, exposure_per_row):
    total_rows = gathered.shape[1]
    count = x.shape[0] // (Q + LAGS)
    step_q = 8
    return pl.pallas_call(
        functools.partial(correlate_kernel, step_q),
        grid=(Q // step_q,),
        out_shape=jax.ShapeDtypeStruct((total_rows, count * LAGS), F32),
        in_specs=[
            pl.BlockSpec((1, total_rows), lambda s: (0, 0)),
            pl.BlockSpec(x.shape, lambda s: (0, 0)),
            pl.BlockSpec((step_q, total_rows, R), lambda s: (s, 0, 0)),
        ],
        out_specs=pl.BlockSpec((total_rows, count * LAGS), lambda s: (0, 0)),
        scratch_shapes=[pltpu.VMEM((total_rows // 128, LAGS * count, 128), F32)],
        compiler_params=pltpu.CompilerParams(vmem_limit_bytes=40 * 2**20),
        name="correlate",
    )(exposure_per_row.reshape(1, total_rows), x, gathered)


def mean_kernel(n, part_ref, mean_ref, slots, own_mean, send_sem, recv_sem):
    me = lax.axis_index("blk")
    barrier = pltpu.get_barrier_semaphore()

    def greet(o, _):
        pl.semaphore_signal(
            barrier, inc=1, device_id={"blk": lax.rem(me + o, n)}, device_id_type=MESH
        )
        return 0

    lax.fori_loop(1, n, greet, 0)
    pl.semaphore_wait(barrier, n - 1)

    def part_copy(o):
        to = lax.rem(me + o, n)
        return pltpu.make_async_remote_copy(
            src_ref=part_ref.at[to],
            dst_ref=slots.at[o],
            send_sem=send_sem.at[0, o],
            recv_sem=recv_sem.at[0, o],
            device_id={"blk": to},
            device_id_type=MESH,
        )

    def mean_copy(o):
        return pltpu.make_async_remote_copy(
            src_ref=own_mean,
            dst_ref=mean_ref.at[me],
            send_sem=send_sem.at[1, o],
            recv_sem=recv_sem.at[1, o],
            device_id={"blk": lax.rem(me + o, n)},
            device_id_type=MESH,
        )

    for o in range(1, n):
        part_copy(o).start()
    total = part_ref[me]
    for o in range(1, n):
        part_copy(o).wait_recv()
        total = total + slots[o]
    own_mean[...] = total[0] / jnp.maximum(total[1], 1.0)
    for o in range(1, n):
        mean_copy(o).start()
    mean_ref[me] = own_mean[...]
    for o in range(1, n):
        mean_copy(o).wait_recv()
    for o in range(1, n):
        part_copy(o).wait_send()
        mean_copy(o).wait_send()


def column_means(sums, counts, n):
    part = jnp.stack([sums.reshape(n, -1, 128), counts.reshape(n, -1, 128)], axis=1)
    share = part.shape[2]
    mean = pl.pallas_call(
        functools.partial(mean_kernel, n),
        out_shape=jax.ShapeDtypeStruct((n, share, 128), F32),
        in_specs=[pl.BlockSpec(memory_space=pltpu.VMEM)],
        out_specs=pl.BlockSpec(memory_space=pltpu.VMEM),
        scratch_shapes=[
            pltpu.VMEM((n, 2, share, 128), F32),
            pltpu.VMEM((share, 128), F32),
            pltpu.SemaphoreType.DMA((2, n)),
            pltpu.SemaphoreType.DMA((2, n)),
        ],
        compiler_params=pltpu.CompilerParams(collective_id=0, has_side_effects=True),
        name="column_means",
    )(part)
    return mean.reshape(-1)


def gather_kernel(chunks, ready_ref, x_ref, acc_ref, held, send_sem, recv_sem):
    me = lax.axis_index("blk")
    z, y, c = me // 4, (me // 2) % 2, me % 2
    span = Q // chunks
    count = x_ref.shape[0] // (Q + LAGS)
    rows = ready_ref.shape[1]
    planes, total_rows = 4, 16 * rows
    tile = 256

    def blk(zz, yy, cc):
        return (zz * 2 + yy) * 2 + cc

    up, down = blk(z + 1, y, c), blk(z - 1, y, c)
    beside, twin = blk(z, 1 - y, c), blk(z, y, 1 - c)

    barrier = pltpu.get_barrier_semaphore()

    def greet(to):
        pl.semaphore_signal(barrier, inc=1, device_id={"blk": to}, device_id_type=MESH)

    greet(beside)
    greet(twin)
    pl.when(z < planes - 1)(lambda: greet(up))
    pl.when(z > 0)(lambda: greet(down))
    held[me] = ready_ref[...]
    acc_ref[...] = jnp.zeros_like(acc_ref)
    inner = (z > 0).astype(jnp.int32) + (z < planes - 1).astype(jnp.int32)
    pl.semaphore_wait(barrier, 2 + inner)

    def copy(source, k, slot, to):
        part = held.at[source, pl.ds(k * span, span)]
        return pltpu.make_async_remote_copy(
            src_ref=part,
            dst_ref=part,
            send_sem=send_sem.at[slot, k],
            recv_sem=recv_sem.at[source, k],
            device_id={"blk": to},
            device_id_type=MESH,
        )

    def z_part(h, k, sign, finish):
        zs = z - sign * h
        source = blk(zs, y, c)

        def go():
            if h > 0 and not finish:
                copy(source, k, 0, twin).wait_recv()

            def act(slot, to):
                one = copy(source, k, slot, to)
                if finish:
                    one.wait_send()
                else:
                    one.start()

            act(8 + zs, beside)
            if sign > 0 or h == 0:
                pl.when(z < planes - 1)(lambda: act(zs, up))
            if sign < 0 or h == 0:
                pl.when(z > 0)(lambda: act(4 + zs, down))
            act(12 + zs, twin)

        if h == 0:
            go()
        else:
            pl.when((zs >= 0) & (zs < planes))(go)

    def y_part(h, k, sign, finish):
        zs = z - sign * h
        source = blk(zs, 1 - y, c)

        def go():
            one = copy(source, k, 16 + zs, twin)
            if finish:
                one.wait_send()
            else:
                one.wait_recv()
                one.start()

        if h == 0:
            go()
        else:
            pl.when((zs >= 0) & (zs < planes))(go)

    def each_hop(part, k_of, finish):
        for h in range(planes):
            k = k_of(h)

            @pl.when((k >= 0) & (k < chunks))
            def _():
                part(h, k, 1, finish)
                if h > 0:
                    part(h, k, -1, finish)

    def product(k):
        for zy in range(2 * planes):
            copy(zy * 2 + 1 - c, k, 0, twin).wait_recv()
        right = jnp.concatenate(
            [held[:, k * span + i].reshape(total_rows, R) for i in range(span)], axis=1
        )

        def one_tile(m, _):
            left = jnp.concatenate(
                [
                    x_ref[pl.ds(pl.multiple_of((k * span + i) * count + m * tile, 16), tile), :]
                    for i in range(span)
                ],
                axis=1,
            )
            acc_ref[pl.ds(pl.multiple_of(m * tile, tile), tile), :] += lax.dot_general(
                left, right, NT_DIMS, preferred_element_type=F32
            )
            return 0

        for m in range(LAGS * count // tile):
            one_tile(m, 0)

    lag = planes + 1

    def step(s, _):
        each_hop(z_part, lambda h: s - h, False)
        each_hop(y_part, lambda h: s - h - 1, False)
        pl.when(s >= lag)(lambda: product(s - lag))
        return 0

    lax.fori_loop(0, chunks + lag, step, 0)

    def finish(k, _):
        each_hop(z_part, lambda h: k, True)
        each_hop(y_part, lambda h: k, True)
        return 0

    lax.fori_loop(0, chunks, finish, 0)


def gather_correlate(x, ready):
    rows = ready.shape[1]
    count = x.shape[0] // (Q + LAGS)
    chunks = 8
    return pl.pallas_call(
        functools.partial(gather_kernel, chunks),
        out_shape=jax.ShapeDtypeStruct((LAGS * count, 16 * rows), F32),
        in_specs=[pl.BlockSpec(memory_space=pltpu.VMEM)] * 2,
        out_specs=pl.BlockSpec(memory_space=pltpu.VMEM),
        scratch_shapes=[
            pltpu.VMEM((16, Q, rows, R), BF16),
            pltpu.SemaphoreType.DMA((20, chunks)),
            pltpu.SemaphoreType.DMA((16, chunks)),
        ],
        compiler_params=pltpu.CompilerParams(
            collective_id=1, has_side_effects=True, vmem_limit_bytes=40 * 2**20
        ),
        name="gather_correlate",
    )(ready, x)


def place_kernel(rows_ref, acc_ref, out_ref, split):
    total_rows = rows_ref.shape[1]
    count = acc_ref.shape[0] // LAGS
    for h in range(total_rows // 128):
        split[h] = acc_ref[:, 128 * h : 128 * (h + 1)]
    place_rows(rows_ref, split, out_ref, count)


def place(acc, exposure_per_row):
    total_rows = acc.shape[1]
    return pl.pallas_call(
        place_kernel,
        out_shape=jax.ShapeDtypeStruct((total_rows, acc.shape[0]), F32),
        in_specs=[pl.BlockSpec(memory_space=pltpu.VMEM)] * 2,
        out_specs=pl.BlockSpec(memory_space=pltpu.VMEM),
        scratch_shapes=[pltpu.VMEM((total_rows // 128, acc.shape[0], 128), F32)],
        compiler_params=pltpu.CompilerParams(vmem_limit_bytes=16 * 2**20),
        name="place",
    )(exposure_per_row.reshape(1, total_rows), acc)


def shards(
    devices,
    observed,
    good_pixel_mask,
    templates,
    template_kernel_index,
    line_spread_table,
    exposure_per_row,
):
    rows = observed.shape[0]
    ring = devices == 16 and rows % 16 == 0
    x = shape_templates(templates, template_kernel_index, line_spread_table)
    good = good_pixel_mask > 0
    flux = jnp.where(good, observed, 0).astype(F32)
    present = (flux > 0).astype(F32)
    sums, counts = jnp.sum(flux, axis=0), jnp.sum(present, axis=0)
    if ring:
        mean = column_means(sums, counts, devices)
    else:
        sums = lax.psum(jnp.stack([sums, counts]), "blk")
        mean = sums[0] / jnp.maximum(sums[1], 1.0)
    resid = present * (flux - mean[None, :])
    scale = lax.rsqrt(jnp.sum(resid * resid, axis=1) / PIX + 1e-06)
    ready = (resid * scale[:, None]).astype(BF16)
    ready = ready.reshape(rows, R, Q).transpose(2, 0, 1)
    if ring:
        return place(gather_correlate(x, ready), exposure_per_row)
    gathered = lax.all_gather(ready, "blk", axis=1, tiled=True)
    return correlate(x, gathered, exposure_per_row)


def solution(mesh):
    in_specs = (
        P(("grp", "blk"), None),
        P(("grp", "blk"), None),
        P(("grp", "blk"), None),
        P(("grp", "blk")),
        P(),
        P("grp"),
    )
    out_specs = P("grp", "blk")
    return jax.shard_map(
        functools.partial(shards, mesh.shape["blk"]),
        mesh=mesh,
        in_specs=in_specs,
        out_specs=out_specs,
        check_vma=False,
    )
```

```python
import functools
import math

import jax
import jax.numpy as jnp
from jax import lax
from jax.experimental import pallas as pl
from jax.experimental.pallas import tpu as pltpu
from jax.sharding import PartitionSpec as P

PIX = 16384
LAGS = 64
TAPS = 97
KERNELS = 8
Q = 128
R = PIX // Q
BAND = 640
CHUNKS = 8
AHEAD = 1
F32 = jnp.float32
BF16 = jnp.bfloat16
MESH = pl.DeviceIdType.MESH
NT_DIMS = (((1,), (1,)), ((), ()))


def template_kernel(index_ref, table_ref, templates_ref, x_ref, bands, chunks, smooth):
    count = templates_ref.shape[0]
    spread_templates(table_ref, templates_ref, bands, chunks)
    smooth_templates(index_ref, bands, chunks, smooth, 0, count, count)
    pack_templates(smooth, x_ref, count)


def spread_templates(table_ref, templates_ref, bands, chunks):
    count = templates_ref.shape[0]
    for k in range(KERNELS):
        row = jnp.broadcast_to(table_ref[k : k + 1, :], (Q, BAND))
        band = pltpu.roll(row, 0, 1, stride=4, stride_axis=0)
        high = band.astype(BF16)
        bands[k, :, :BAND] = high
        bands[k, :, BAND:] = (band - high.astype(F32)).astype(BF16)

    def spread(r, _):
        at = pl.multiple_of(r * (4 * Q), 128)
        piece = templates_ref[:, pl.ds(at, BAND)].astype(F32)
        for i in range(BAND // 128):
            chunks[i, pl.ds(pl.multiple_of(r * count, count), count), :] = piece[
                :, 128 * i : 128 * (i + 1)
            ]
        return 0

    lax.fori_loop(0, R - 1, spread, 0, unroll=8)
    last = (R - 1) * 4 * Q
    left = templates_ref.shape[1] - last
    tail = templates_ref[:, last:].astype(F32)
    tail = jnp.concatenate([tail, jnp.zeros((count, BAND - left), F32)], axis=1)
    for i in range(BAND // 128):
        chunks[i, (R - 1) * count :, :] = tail[:, 128 * i : 128 * (i + 1)]


def smooth_templates(index_ref, bands, chunks, smooth, first, last, count):
    for t in range(first, last):
        rows = [
            chunks[i, pl.ds(t, R, stride=count), :].astype(BF16) for i in range(BAND // 128)
        ]
        rows = jnp.concatenate(rows + rows, axis=1)
        flux = lax.dot_general(
            bands[index_ref[t]], rows, NT_DIMS, preferred_element_type=F32
        )
        total = jnp.sum(flux * flux)
        smooth[pl.ds(t, Q, stride=count), :] = flux * lax.rsqrt(
            jnp.full((1, 1), total) / PIX + 1e-06
        )


def pack_templates(smooth, x_ref, count):
    half = LAGS // 2
    body = smooth[...]
    lane = lax.broadcasted_iota(jnp.int32, (half * count, R), 1)
    x_ref[half * count : (half + Q) * count, :] = body.astype(BF16)
    before = pltpu.roll(body[(Q - half) * count :, :], 1, 1)
    x_ref[: half * count, :] = jnp.where(lane == 0, 0.0, before).astype(BF16)
    after = pltpu.roll(body[: half * count, :], R - 1, 1)
    x_ref[(half + Q) * count :, :] = jnp.where(lane == R - 1, 0.0, after).astype(BF16)


def shape_templates(templates, template_kernel_index, line_spread_table):
    count = templates.shape[0]
    table = jnp.pad(line_spread_table, ((0, 0), (0, BAND - TAPS)))
    return pl.pallas_call(
        template_kernel,
        out_shape=jax.ShapeDtypeStruct(((Q + LAGS) * count, R), BF16),
        in_specs=[
            pl.BlockSpec(memory_space=pltpu.SMEM),
            pl.BlockSpec(memory_space=pltpu.VMEM),
            pl.BlockSpec(memory_space=pltpu.VMEM),
        ],
        out_specs=pl.BlockSpec(memory_space=pltpu.VMEM),
        scratch_shapes=[
            pltpu.VMEM((KERNELS, Q, 2 * BAND), BF16),
            pltpu.VMEM((BAND // 128, R * count, 128), F32),
            pltpu.VMEM((Q * count, R), F32),
        ],
        compiler_params=pltpu.CompilerParams(vmem_limit_bytes=40 * 2**20),
        cost_estimate=pl.CostEstimate(
            flops=2 * count * Q * R * 2 * BAND, bytes_accessed=6 * 2**20, transcendentals=0
        ),
        name="shape_templates",
    )(template_kernel_index, table, templates)


def place_rows(rows_ref, acc, out_ref, count):
    total_rows = rows_ref.shape[1]
    chosen = (
        lax.broadcasted_iota(jnp.int32, (total_rows, total_rows), 0) == rows_ref[...]
    ).astype(BF16)
    both = jnp.concatenate([chosen, chosen], axis=1)
    for t in range(0, count, 2):
        part = jnp.concatenate(
            [
                jnp.concatenate(
                    [
                        acc[h, pl.ds(t + i, LAGS, stride=count), :]
                        for h in range(total_rows // 128)
                    ],
                    axis=1,
                )
                for i in range(2)
            ],
            axis=0,
        ) * F32(1.0 / math.sqrt(PIX))
        high = part.astype(BF16)
        low = (part - high.astype(F32)).astype(BF16)
        out_ref[:, t * LAGS : (t + 2) * LAGS] = lax.dot_general(
            both,
            jnp.concatenate([high, low], axis=1),
            NT_DIMS,
            preferred_element_type=F32,
        )


def correlate_kernel(step_q, rows_ref, x_ref, g_ref, out_ref, acc):
    step = pl.program_id(0)
    total_rows = rows_ref.shape[1]
    count = x_ref.shape[0] // (Q + LAGS)
    tile = 256

    @pl.when(step == 0)
    def _():
        acc[...] = jnp.zeros_like(acc)

    right = jnp.concatenate([g_ref[i] for i in range(step_q)], axis=1)
    for m in range(LAGS * count // tile):
        left = jnp.concatenate(
            [
                x_ref[pl.ds(pl.multiple_of((step * step_q + i) * count + m * tile, 16), tile), :]
                for i in range(step_q)
            ],
            axis=1,
        )
        part = lax.dot_general(left, right, NT_DIMS, preferred_element_type=F32)
        for h in range(total_rows // 128):
            acc[h, m * tile : (m + 1) * tile, :] += part[:, 128 * h : 128 * (h + 1)]

    @pl.when(step == pl.num_programs(0) - 1)
    def _():
        place_rows(rows_ref, acc, out_ref, count)


def correlate(x, gathered, exposure_per_row):
    total_rows = gathered.shape[1]
    count = x.shape[0] // (Q + LAGS)
    step_q = 8
    return pl.pallas_call(
        functools.partial(correlate_kernel, step_q),
        grid=(Q // step_q,),
        out_shape=jax.ShapeDtypeStruct((total_rows, count * LAGS), F32),
        in_specs=[
            pl.BlockSpec((1, total_rows), lambda s: (0, 0)),
            pl.BlockSpec(x.shape, lambda s: (0, 0)),
            pl.BlockSpec((step_q, total_rows, R), lambda s: (s, 0, 0)),
        ],
        out_specs=pl.BlockSpec((total_rows, count * LAGS), lambda s: (0, 0)),
        scratch_shapes=[pltpu.VMEM((total_rows // 128, LAGS * count, 128), F32)],
        compiler_params=pltpu.CompilerParams(vmem_limit_bytes=40 * 2**20),
        name="correlate",
    )(exposure_per_row.reshape(1, total_rows), x, gathered)


def mean_kernel(
    n,
    part_ref,
    index_ref,
    table_ref,
    templates_ref,
    mean_ref,
    x_ref,
    slots,
    own_mean,
    send_sem,
    recv_sem,
    bands,
    chunks,
    smooth,
):
    count = templates_ref.shape[0]
    me = lax.axis_index("blk")
    barrier = pltpu.get_barrier_semaphore()

    def greet(o, _):
        pl.semaphore_signal(
            barrier, inc=1, device_id={"blk": lax.rem(me + o, n)}, device_id_type=MESH
        )
        return 0

    lax.fori_loop(1, n, greet, 0)
    pl.semaphore_wait(barrier, n - 1)

    def part_copy(o):
        to = lax.rem(me + o, n)
        return pltpu.make_async_remote_copy(
            src_ref=part_ref.at[to],
            dst_ref=slots.at[o],
            send_sem=send_sem.at[0, o],
            recv_sem=recv_sem.at[0, o],
            device_id={"blk": to},
            device_id_type=MESH,
        )

    def mean_copy(o):
        return pltpu.make_async_remote_copy(
            src_ref=own_mean,
            dst_ref=mean_ref.at[me],
            send_sem=send_sem.at[1, o],
            recv_sem=recv_sem.at[1, o],
            device_id={"blk": lax.rem(me + o, n)},
            device_id_type=MESH,
        )

    for o in range(1, n):
        part_copy(o).start()
    spread_templates(table_ref, templates_ref, bands, chunks)
    smooth_templates(index_ref, bands, chunks, smooth, 0, count // 2, count)
    total = part_ref[me]
    for o in range(1, n):
        part_copy(o).wait_recv()
        total = total + slots[o]
    own_mean[...] = total[0] / jnp.maximum(total[1], 1.0)
    for o in range(1, n):
        mean_copy(o).start()
    mean_ref[me] = own_mean[...]
    smooth_templates(index_ref, bands, chunks, smooth, count // 2, count, count)
    pack_templates(smooth, x_ref, count)
    for o in range(1, n):
        mean_copy(o).wait_recv()
    for o in range(1, n):
        part_copy(o).wait_send()
        mean_copy(o).wait_send()


def column_means(sums, counts, n, templates, template_kernel_index, line_spread_table):
    part = jnp.stack([sums.reshape(n, -1, 128), counts.reshape(n, -1, 128)], axis=1)
    share = part.shape[2]
    count = templates.shape[0]
    table = jnp.pad(line_spread_table, ((0, 0), (0, BAND - TAPS)))
    mean, x = pl.pallas_call(
        functools.partial(mean_kernel, n),
        out_shape=(
            jax.ShapeDtypeStruct((n, share, 128), F32),
            jax.ShapeDtypeStruct(((Q + LAGS) * count, R), BF16),
        ),
        in_specs=[
            pl.BlockSpec(memory_space=pltpu.VMEM),
            pl.BlockSpec(memory_space=pltpu.SMEM),
            pl.BlockSpec(memory_space=pltpu.VMEM),
            pl.BlockSpec(memory_space=pltpu.VMEM),
        ],
        out_specs=(pl.BlockSpec(memory_space=pltpu.VMEM), pl.BlockSpec(memory_space=pltpu.VMEM)),
        scratch_shapes=[
            pltpu.VMEM((n, 2, share, 128), F32),
            pltpu.VMEM((share, 128), F32),
            pltpu.SemaphoreType.DMA((2, n)),
            pltpu.SemaphoreType.DMA((2, n)),
            pltpu.VMEM((KERNELS, Q, 2 * BAND), BF16),
            pltpu.VMEM((BAND // 128, R * count, 128), F32),
            pltpu.VMEM((Q * count, R), F32),
        ],
        compiler_params=pltpu.CompilerParams(
            collective_id=0, has_side_effects=True, vmem_limit_bytes=40 * 2**20
        ),
        name="column_means",
    )(part, template_kernel_index, table, templates)
    return mean.reshape(-1), x


def gather_kernel(chunks, ready_ref, x_ref, acc_ref, held, send_sem, recv_sem):
    me = lax.axis_index("blk")
    z, y, c = me // 4, (me // 2) % 2, me % 2
    span = Q // chunks
    count = x_ref.shape[0] // (Q + LAGS)
    rows = ready_ref.shape[1]
    planes, total_rows = 4, 16 * rows
    tile = 256

    def blk(zz, yy, cc):
        return (zz * 2 + yy) * 2 + cc

    up, down = blk(z + 1, y, c), blk(z - 1, y, c)
    beside, twin = blk(z, 1 - y, c), blk(z, y, 1 - c)

    middle = (z == 1) | (z == 2)
    barrier = pltpu.get_barrier_semaphore()

    def greet(to):
        pl.semaphore_signal(barrier, inc=1, device_id={"blk": to}, device_id_type=MESH)

    greet(beside)
    greet(twin)
    pl.when(z < planes - 1)(lambda: greet(up))
    pl.when(z > 0)(lambda: greet(down))
    held[me] = ready_ref[...]
    acc_ref[...] = jnp.zeros_like(acc_ref)
    inner = (z > 0).astype(jnp.int32) + (z < planes - 1).astype(jnp.int32)
    pl.semaphore_wait(barrier, 2 + inner)

    def copy(source, k, slot, to):
        part = held.at[source, pl.ds(k * span, span)]
        return pltpu.make_async_remote_copy(
            src_ref=part,
            dst_ref=part,
            send_sem=send_sem.at[slot, k],
            recv_sem=recv_sem.at[source, k],
            device_id={"blk": to},
            device_id_type=MESH,
        )

    def z_part(h, k, sign, finish):
        zs = z - sign * h
        source = blk(zs, y, c)

        def go():
            if h > 0 and not finish:
                copy(source, k, 0, twin).wait_recv()

            def act(slot, to):
                one = copy(source, k, slot, to)
                if finish:
                    one.wait_send()
                else:
                    one.start()

            skip = (zs == 3 * (1 - z % 2)) & (middle | (k % 2 == 1))
            pl.when(jnp.logical_not(skip))(lambda: act(8 + zs, beside))
            if sign > 0 or h == 0:
                pl.when(z < planes - 1)(lambda: act(zs, up))
            if sign < 0 or h == 0:
                pl.when(z > 0)(lambda: act(4 + zs, down))
            act(12 + zs, twin)

        if h == 0:
            go()
        else:
            pl.when((zs >= 0) & (zs < planes))(go)

    def y_part(h, k, sign, finish):
        zs = z - sign * h
        source = blk(zs, 1 - y, c)

        def go():
            one = copy(source, k, 16 + zs, twin)
            along = copy(source, k, 20, jnp.where(z % 2 == 0, up, down))
            passes = (zs == 3 * (z % 2)) & (jnp.logical_not(middle) | (k % 2 == 1))
            if finish:
                one.wait_send()
                pl.when(passes)(lambda: along.wait_send())
            else:
                one.wait_recv()
                pl.when(passes)(lambda: along.start())
                one.start()

        if h == 0:
            go()
        else:
            pl.when((zs >= 0) & (zs < planes))(go)

    def each_hop(part, k_of, finish):
        for h in range(planes):
            k = k_of(h)

            @pl.when((k >= 0) & (k < chunks))
            def _():
                part(h, k, 1, finish)
                if h > 0:
                    part(h, k, -1, finish)

    def product(k):
        for zy in range(2 * planes):
            copy(zy * 2 + 1 - c, k, 0, twin).wait_recv()
        right = jnp.concatenate(
            [held[:, k * span + i].reshape(total_rows, R) for i in range(span)], axis=1
        )

        def one_tile(m, _):
            left = jnp.concatenate(
                [
                    x_ref[pl.ds(pl.multiple_of((k * span + i) * count + m * tile, 16), tile), :]
                    for i in range(span)
                ],
                axis=1,
            )
            acc_ref[pl.ds(pl.multiple_of(m * tile, tile), tile), :] += lax.dot_general(
                left, right, NT_DIMS, preferred_element_type=F32
            )
            return 0

        for m in range(LAGS * count // tile):
            one_tile(m, 0)

    lag = planes + 1 + AHEAD

    def step(s, _):
        each_hop(z_part, lambda h: s - h - (AHEAD if h > 0 else 0), False)
        each_hop(y_part, lambda h: s - h - 1 - AHEAD, False)
        pl.when(s >= lag)(lambda: product(s - lag))
        return 0

    lax.fori_loop(0, chunks + lag, step, 0)

    def finish(k, _):
        each_hop(z_part, lambda h: k, True)
        each_hop(y_part, lambda h: k, True)
        return 0

    lax.fori_loop(0, chunks, finish, 0)


def gather_correlate(x, ready):
    rows = ready.shape[1]
    count = x.shape[0] // (Q + LAGS)
    chunks = CHUNKS
    return pl.pallas_call(
        functools.partial(gather_kernel, chunks),
        out_shape=jax.ShapeDtypeStruct((LAGS * count, 16 * rows), F32),
        in_specs=[pl.BlockSpec(memory_space=pltpu.VMEM)] * 2,
        out_specs=pl.BlockSpec(memory_space=pltpu.VMEM),
        scratch_shapes=[
            pltpu.VMEM((16, Q, rows, R), BF16),
            pltpu.SemaphoreType.DMA((21, chunks)),
            pltpu.SemaphoreType.DMA((16, chunks)),
        ],
        compiler_params=pltpu.CompilerParams(
            collective_id=1, has_side_effects=True, vmem_limit_bytes=40 * 2**20
        ),
        name="gather_correlate",
    )(ready, x)


def place_kernel(rows_ref, acc_ref, out_ref, split):
    total_rows = rows_ref.shape[1]
    count = acc_ref.shape[0] // LAGS
    for h in range(total_rows // 128):
        split[h] = acc_ref[:, 128 * h : 128 * (h + 1)]
    place_rows(rows_ref, split, out_ref, count)


def place(acc, exposure_per_row):
    total_rows = acc.shape[1]
    return pl.pallas_call(
        place_kernel,
        out_shape=jax.ShapeDtypeStruct((total_rows, acc.shape[0]), F32),
        in_specs=[pl.BlockSpec(memory_space=pltpu.VMEM)] * 2,
        out_specs=pl.BlockSpec(memory_space=pltpu.VMEM),
        scratch_shapes=[pltpu.VMEM((total_rows // 128, acc.shape[0], 128), F32)],
        compiler_params=pltpu.CompilerParams(vmem_limit_bytes=16 * 2**20),
        name="place",
    )(exposure_per_row.reshape(1, total_rows), acc)


def shards(
    devices,
    observed,
    good_pixel_mask,
    templates,
    template_kernel_index,
    line_spread_table,
    exposure_per_row,
):
    rows = observed.shape[0]
    ring = devices == 16 and rows % 16 == 0
    good = good_pixel_mask > 0
    flux = jnp.where(good, observed, 0).astype(F32)
    present = (flux > 0).astype(F32)
    sums, counts = jnp.sum(flux, axis=0), jnp.sum(present, axis=0)
    if ring:
        mean, x = column_means(
            sums, counts, devices, templates, template_kernel_index, line_spread_table
        )
    else:
        x = shape_templates(templates, template_kernel_index, line_spread_table)
        sums = lax.psum(jnp.stack([sums, counts]), "blk")
        mean = sums[0] / jnp.maximum(sums[1], 1.0)
    resid = present * (flux - mean[None, :])
    scale = lax.rsqrt(jnp.sum(resid * resid, axis=1) / PIX + 1e-06)
    ready = (resid * scale[:, None]).astype(BF16)
    ready = ready.reshape(rows, R, Q).transpose(2, 0, 1)
    if ring:
        return place(gather_correlate(x, ready), exposure_per_row)
    gathered = lax.all_gather(ready, "blk", axis=1, tiled=True)
    return correlate(x, gathered, exposure_per_row)


def solution(mesh):
    in_specs = (
        P(("grp", "blk"), None),
        P(("grp", "blk"), None),
        P(("grp", "blk"), None),
        P(("grp", "blk")),
        P(),
        P("grp"),
    )
    out_specs = P("grp", "blk")
    return jax.shard_map(
        functools.partial(shards, mesh.shape["blk"]),
        mesh=mesh,
        in_specs=in_specs,
        out_specs=out_specs,
        check_vma=False,
    )
```

```python
import functools
import math

import jax
import jax.numpy as jnp
from jax import lax
from jax.experimental import pallas as pl
from jax.experimental.pallas import tpu as pltpu
from jax.sharding import PartitionSpec as P

PIX = 16384
LAGS = 64
TAPS = 97
KERNELS = 8
Q = 128
R = PIX // Q
BAND = 640
CHUNKS = 8
AHEAD = 1
F32 = jnp.float32
BF16 = jnp.bfloat16
MESH = pl.DeviceIdType.MESH
NT_DIMS = (((1,), (1,)), ((), ()))


def template_kernel(index_ref, table_ref, templates_ref, x_ref, bands, chunks, smooth):
    count = templates_ref.shape[0]
    spread_templates(table_ref, templates_ref, bands, chunks)
    smooth_templates(index_ref, bands, chunks, smooth, 0, count, count)
    pack_templates(smooth, x_ref, count)


def spread_templates(table_ref, templates_ref, bands, chunks):
    count = templates_ref.shape[0]
    for k in range(KERNELS):
        row = jnp.concatenate(
            [table_ref[k : k + 1, :], jnp.zeros((1, BAND - TAPS), F32)], axis=1
        )
        row = jnp.broadcast_to(row, (Q, BAND))
        band = pltpu.roll(row, 0, 1, stride=4, stride_axis=0)
        high = band.astype(BF16)
        bands[k, :, :BAND] = high
        bands[k, :, BAND:] = (band - high.astype(F32)).astype(BF16)

    def spread(r, _):
        at = pl.multiple_of(r * (4 * Q), 128)
        piece = templates_ref[:, pl.ds(at, BAND)].astype(F32)
        for i in range(BAND // 128):
            chunks[i, pl.ds(pl.multiple_of(r * count, count), count), :] = piece[
                :, 128 * i : 128 * (i + 1)
            ]
        return 0

    lax.fori_loop(0, R - 1, spread, 0, unroll=8)
    last = (R - 1) * 4 * Q
    left = templates_ref.shape[1] - last
    tail = templates_ref[:, last:].astype(F32)
    tail = jnp.concatenate([tail, jnp.zeros((count, BAND - left), F32)], axis=1)
    for i in range(BAND // 128):
        chunks[i, (R - 1) * count :, :] = tail[:, 128 * i : 128 * (i + 1)]


def smooth_templates(index_ref, bands, chunks, smooth, first, last, count):
    for t in range(first, last):
        rows = [
            chunks[i, pl.ds(t, R, stride=count), :].astype(BF16) for i in range(BAND // 128)
        ]
        rows = jnp.concatenate(rows + rows, axis=1)
        flux = lax.dot_general(
            bands[index_ref[t]], rows, NT_DIMS, preferred_element_type=F32
        )
        total = jnp.sum(flux * flux)
        smooth[pl.ds(t, Q, stride=count), :] = flux * lax.rsqrt(
            jnp.full((1, 1), total) / PIX + 1e-06
        )


def pack_templates(smooth, x_ref, count):
    half = LAGS // 2
    body = smooth[...]
    lane = lax.broadcasted_iota(jnp.int32, (half * count, R), 1)
    x_ref[half * count : (half + Q) * count, :] = body.astype(BF16)
    before = pltpu.roll(body[(Q - half) * count :, :], 1, 1)
    x_ref[: half * count, :] = jnp.where(lane == 0, 0.0, before).astype(BF16)
    after = pltpu.roll(body[: half * count, :], R - 1, 1)
    x_ref[(half + Q) * count :, :] = jnp.where(lane == R - 1, 0.0, after).astype(BF16)


def shape_templates(templates, template_kernel_index, line_spread_table):
    count = templates.shape[0]
    return pl.pallas_call(
        template_kernel,
        out_shape=jax.ShapeDtypeStruct(((Q + LAGS) * count, R), BF16),
        in_specs=[
            pl.BlockSpec(memory_space=pltpu.SMEM),
            pl.BlockSpec(memory_space=pltpu.VMEM),
            pl.BlockSpec(memory_space=pltpu.VMEM),
        ],
        out_specs=pl.BlockSpec(memory_space=pltpu.VMEM),
        scratch_shapes=[
            pltpu.VMEM((KERNELS, Q, 2 * BAND), BF16),
            pltpu.VMEM((BAND // 128, R * count, 128), F32),
            pltpu.VMEM((Q * count, R), F32),
        ],
        compiler_params=pltpu.CompilerParams(vmem_limit_bytes=40 * 2**20),
        cost_estimate=pl.CostEstimate(
            flops=2 * count * Q * R * 2 * BAND, bytes_accessed=6 * 2**20, transcendentals=0
        ),
        name="shape_templates",
    )(template_kernel_index, line_spread_table, templates)


def place_rows(rows_ref, acc, out_ref, count):
    total_rows = rows_ref.shape[1]
    chosen = (
        lax.broadcasted_iota(jnp.int32, (total_rows, total_rows), 0) == rows_ref[...]
    ).astype(BF16)
    both = jnp.concatenate([chosen, chosen], axis=1)
    for t in range(0, count, 2):
        part = jnp.concatenate(
            [
                jnp.concatenate(
                    [
                        acc[h, pl.ds(t + i, LAGS, stride=count), :]
                        for h in range(total_rows // 128)
                    ],
                    axis=1,
                )
                for i in range(2)
            ],
            axis=0,
        ) * F32(1.0 / math.sqrt(PIX))
        high = part.astype(BF16)
        low = (part - high.astype(F32)).astype(BF16)
        out_ref[:, t * LAGS : (t + 2) * LAGS] = lax.dot_general(
            both,
            jnp.concatenate([high, low], axis=1),
            NT_DIMS,
            preferred_element_type=F32,
        )


def correlate_kernel(step_q, rows_ref, x_ref, g_ref, out_ref, acc):
    step = pl.program_id(0)
    total_rows = rows_ref.shape[1]
    count = x_ref.shape[0] // (Q + LAGS)
    tile = 256

    @pl.when(step == 0)
    def _():
        acc[...] = jnp.zeros_like(acc)

    right = jnp.concatenate([g_ref[i] for i in range(step_q)], axis=1)
    for m in range(LAGS * count // tile):
        left = jnp.concatenate(
            [
                x_ref[pl.ds(pl.multiple_of((step * step_q + i) * count + m * tile, 16), tile), :]
                for i in range(step_q)
            ],
            axis=1,
        )
        part = lax.dot_general(left, right, NT_DIMS, preferred_element_type=F32)
        for h in range(total_rows // 128):
            acc[h, m * tile : (m + 1) * tile, :] += part[:, 128 * h : 128 * (h + 1)]

    @pl.when(step == pl.num_programs(0) - 1)
    def _():
        place_rows(rows_ref, acc, out_ref, count)


def correlate(x, gathered, exposure_per_row):
    total_rows = gathered.shape[1]
    count = x.shape[0] // (Q + LAGS)
    step_q = 8
    return pl.pallas_call(
        functools.partial(correlate_kernel, step_q),
        grid=(Q // step_q,),
        out_shape=jax.ShapeDtypeStruct((total_rows, count * LAGS), F32),
        in_specs=[
            pl.BlockSpec((1, total_rows), lambda s: (0, 0)),
            pl.BlockSpec(x.shape, lambda s: (0, 0)),
            pl.BlockSpec((step_q, total_rows, R), lambda s: (s, 0, 0)),
        ],
        out_specs=pl.BlockSpec((total_rows, count * LAGS), lambda s: (0, 0)),
        scratch_shapes=[pltpu.VMEM((total_rows // 128, LAGS * count, 128), F32)],
        compiler_params=pltpu.CompilerParams(vmem_limit_bytes=40 * 2**20),
        name="correlate",
    )(exposure_per_row.reshape(1, total_rows), x, gathered)


def mean_kernel(
    n,
    part_ref,
    index_ref,
    table_ref,
    templates_ref,
    mean_ref,
    x_ref,
    slots,
    own_mean,
    send_sem,
    recv_sem,
    bands,
    chunks,
    smooth,
):
    count = templates_ref.shape[0]
    me = lax.axis_index("blk")
    barrier = pltpu.get_barrier_semaphore()

    def greet(o, _):
        pl.semaphore_signal(
            barrier, inc=1, device_id={"blk": lax.rem(me + o, n)}, device_id_type=MESH
        )
        return 0

    lax.fori_loop(1, n, greet, 0)
    pl.semaphore_wait(barrier, n - 1)

    def part_copy(o):
        to = lax.rem(me + o, n)
        return pltpu.make_async_remote_copy(
            src_ref=part_ref.at[to],
            dst_ref=slots.at[o],
            send_sem=send_sem.at[0, o],
            recv_sem=recv_sem.at[0, o],
            device_id={"blk": to},
            device_id_type=MESH,
        )

    def mean_copy(o):
        return pltpu.make_async_remote_copy(
            src_ref=own_mean,
            dst_ref=mean_ref.at[me],
            send_sem=send_sem.at[1, o],
            recv_sem=recv_sem.at[1, o],
            device_id={"blk": lax.rem(me + o, n)},
            device_id_type=MESH,
        )

    for o in range(1, n):
        part_copy(o).start()
    spread_templates(table_ref, templates_ref, bands, chunks)
    smooth_templates(index_ref, bands, chunks, smooth, 0, count // 2, count)
    total = part_ref[me]
    for o in range(1, n):
        part_copy(o).wait_recv()
        total = total + slots[o]
    own_mean[...] = total[0] / jnp.maximum(total[1], 1.0)
    for o in range(1, n):
        mean_copy(o).start()
    mean_ref[me] = own_mean[...]
    smooth_templates(index_ref, bands, chunks, smooth, count // 2, count, count)
    pack_templates(smooth, x_ref, count)
    for o in range(1, n):
        mean_copy(o).wait_recv()
    for o in range(1, n):
        part_copy(o).wait_send()
        mean_copy(o).wait_send()


def column_means(sums, counts, n, templates, template_kernel_index, line_spread_table):
    part = jnp.stack([sums.reshape(n, -1, 128), counts.reshape(n, -1, 128)], axis=1)
    share = part.shape[2]
    count = templates.shape[0]
    mean, x = pl.pallas_call(
        functools.partial(mean_kernel, n),
        out_shape=(
            jax.ShapeDtypeStruct((n, share, 128), F32),
            jax.ShapeDtypeStruct(((Q + LAGS) * count, R), BF16),
        ),
        in_specs=[
            pl.BlockSpec(memory_space=pltpu.VMEM),
            pl.BlockSpec(memory_space=pltpu.SMEM),
            pl.BlockSpec(memory_space=pltpu.VMEM),
            pl.BlockSpec(memory_space=pltpu.VMEM),
        ],
        out_specs=(pl.BlockSpec(memory_space=pltpu.VMEM), pl.BlockSpec(memory_space=pltpu.VMEM)),
        scratch_shapes=[
            pltpu.VMEM((n, 2, share, 128), F32),
            pltpu.VMEM((share, 128), F32),
            pltpu.SemaphoreType.DMA((2, n)),
            pltpu.SemaphoreType.DMA((2, n)),
            pltpu.VMEM((KERNELS, Q, 2 * BAND), BF16),
            pltpu.VMEM((BAND // 128, R * count, 128), F32),
            pltpu.VMEM((Q * count, R), F32),
        ],
        compiler_params=pltpu.CompilerParams(
            collective_id=0, has_side_effects=True, vmem_limit_bytes=40 * 2**20
        ),
        name="column_means",
    )(part, template_kernel_index, line_spread_table, templates)
    return mean.reshape(-1), x


def gather_kernel(chunks, ready_ref, x_ref, acc_ref, held, send_sem, recv_sem):
    me = lax.axis_index("blk")
    z, y, c = me // 4, (me // 2) % 2, me % 2
    span = Q // chunks
    count = x_ref.shape[0] // (Q + LAGS)
    rows = ready_ref.shape[1]
    planes, total_rows = 4, 16 * rows
    tile = 256

    def blk(zz, yy, cc):
        return (zz * 2 + yy) * 2 + cc

    up, down = blk(z + 1, y, c), blk(z - 1, y, c)
    beside, twin = blk(z, 1 - y, c), blk(z, y, 1 - c)

    middle = (z == 1) | (z == 2)
    barrier = pltpu.get_barrier_semaphore()

    def greet(to):
        pl.semaphore_signal(barrier, inc=1, device_id={"blk": to}, device_id_type=MESH)

    greet(beside)
    greet(twin)
    pl.when(z < planes - 1)(lambda: greet(up))
    pl.when(z > 0)(lambda: greet(down))
    held[me] = ready_ref[...]
    acc_ref[...] = jnp.zeros_like(acc_ref)
    inner = (z > 0).astype(jnp.int32) + (z < planes - 1).astype(jnp.int32)
    pl.semaphore_wait(barrier, 2 + inner)

    def copy(source, k, slot, to):
        part = held.at[source, pl.ds(k * span, span)]
        return pltpu.make_async_remote_copy(
            src_ref=part,
            dst_ref=part,
            send_sem=send_sem.at[slot, k],
            recv_sem=recv_sem.at[source, k],
            device_id={"blk": to},
            device_id_type=MESH,
        )

    def z_part(h, k, sign, finish):
        zs = z - sign * h
        source = blk(zs, y, c)

        def go():
            if h > 0 and not finish:
                copy(source, k, 0, twin).wait_recv()

            def act(slot, to):
                one = copy(source, k, slot, to)
                if finish:
                    one.wait_send()
                else:
                    one.start()

            if sign > 0 or h == 0:
                pl.when(z < planes - 1)(lambda: act(zs, up))
            if sign < 0 or h == 0:
                pl.when(z > 0)(lambda: act(4 + zs, down))
            skip = (zs == 3 * (1 - z % 2)) & (middle | (k % 2 == 1))
            pl.when(jnp.logical_not(skip))(lambda: act(8 + zs, beside))
            act(12 + zs, twin)

        if h == 0:
            go()
        else:
            pl.when((zs >= 0) & (zs < planes))(go)

    def y_part(h, k, sign, finish):
        zs = z - sign * h
        source = blk(zs, 1 - y, c)

        def go():
            one = copy(source, k, 16 + zs, twin)
            along = copy(source, k, 20, jnp.where(z % 2 == 0, up, down))
            passes = (zs == 3 * (z % 2)) & (jnp.logical_not(middle) | (k % 2 == 1))
            if finish:
                one.wait_send()
                pl.when(passes)(lambda: along.wait_send())
            else:
                one.wait_recv()
                pl.when(passes)(lambda: along.start())
                one.start()

        if h == 0:
            go()
        else:
            pl.when((zs >= 0) & (zs < planes))(go)

    def each_hop(part, k_of, finish):
        for h in range(planes):
            k = k_of(h)

            @pl.when((k >= 0) & (k < chunks))
            def _():
                part(h, k, 1, finish)
                if h > 0:
                    part(h, k, -1, finish)

    def product(k):
        for zy in range(2 * planes):
            copy(zy * 2 + 1 - c, k, 0, twin).wait_recv()
        right = jnp.concatenate(
            [held[:, k * span + i].reshape(total_rows, R) for i in range(span)], axis=1
        )

        def one_tile(m, _):
            left = jnp.concatenate(
                [
                    x_ref[pl.ds(pl.multiple_of((k * span + i) * count + m * tile, 16), tile), :]
                    for i in range(span)
                ],
                axis=1,
            )
            acc_ref[pl.ds(pl.multiple_of(m * tile, tile), tile), :] += lax.dot_general(
                left, right, NT_DIMS, preferred_element_type=F32
            )
            return 0

        for m in range(LAGS * count // tile):
            one_tile(m, 0)

    lag = planes + 1 + AHEAD

    def step(s, _):
        each_hop(z_part, lambda h: s - h - (AHEAD if h > 0 else 0), False)
        each_hop(y_part, lambda h: s - h - 1 - AHEAD, False)
        pl.when(s >= lag)(lambda: product(s - lag))
        return 0

    lax.fori_loop(0, chunks + lag, step, 0)

    def finish(k, _):
        each_hop(z_part, lambda h: k, True)
        each_hop(y_part, lambda h: k, True)
        return 0

    lax.fori_loop(0, chunks, finish, 0)


def gather_correlate(x, ready):
    rows = ready.shape[1]
    count = x.shape[0] // (Q + LAGS)
    chunks = CHUNKS
    return pl.pallas_call(
        functools.partial(gather_kernel, chunks),
        out_shape=jax.ShapeDtypeStruct((LAGS * count, 16 * rows), F32),
        in_specs=[pl.BlockSpec(memory_space=pltpu.VMEM)] * 2,
        out_specs=pl.BlockSpec(memory_space=pltpu.VMEM),
        scratch_shapes=[
            pltpu.VMEM((16, Q, rows, R), BF16),
            pltpu.SemaphoreType.DMA((21, chunks)),
            pltpu.SemaphoreType.DMA((16, chunks)),
        ],
        compiler_params=pltpu.CompilerParams(
            collective_id=1, has_side_effects=True, vmem_limit_bytes=40 * 2**20
        ),
        name="gather_correlate",
    )(ready, x)


def place_kernel(rows_ref, acc_ref, out_ref, split):
    total_rows = rows_ref.shape[1]
    count = acc_ref.shape[0] // LAGS
    for h in range(total_rows // 128):
        split[h] = acc_ref[:, 128 * h : 128 * (h + 1)]
    place_rows(rows_ref, split, out_ref, count)


def place(acc, exposure_per_row):
    total_rows = acc.shape[1]
    return pl.pallas_call(
        place_kernel,
        out_shape=jax.ShapeDtypeStruct((total_rows, acc.shape[0]), F32),
        in_specs=[pl.BlockSpec(memory_space=pltpu.VMEM)] * 2,
        out_specs=pl.BlockSpec(memory_space=pltpu.VMEM),
        scratch_shapes=[pltpu.VMEM((total_rows // 128, acc.shape[0], 128), F32)],
        compiler_params=pltpu.CompilerParams(vmem_limit_bytes=16 * 2**20),
        name="place",
    )(exposure_per_row.reshape(1, total_rows), acc)


def shards(
    devices,
    observed,
    good_pixel_mask,
    templates,
    template_kernel_index,
    line_spread_table,
    exposure_per_row,
):
    rows = observed.shape[0]
    ring = devices == 16 and rows % 16 == 0
    good = good_pixel_mask > 0
    flux = jnp.where(good, observed, 0).astype(F32)
    present = (flux > 0).astype(F32)
    sums, counts = jnp.sum(flux, axis=0), jnp.sum(present, axis=0)
    if ring:
        mean, x = column_means(
            sums, counts, devices, templates, template_kernel_index, line_spread_table
        )
    else:
        x = shape_templates(templates, template_kernel_index, line_spread_table)
        sums = lax.psum(jnp.stack([sums, counts]), "blk")
        mean = sums[0] / jnp.maximum(sums[1], 1.0)
    resid = present * (flux - mean[None, :])
    scale = lax.rsqrt(jnp.sum(resid * resid, axis=1) / PIX + 1e-06)
    ready = (resid * scale[:, None]).astype(BF16)
    ready = ready.reshape(rows, R, Q).transpose(2, 0, 1)
    if ring:
        return place(gather_correlate(x, ready), exposure_per_row)
    gathered = lax.all_gather(ready, "blk", axis=1, tiled=True)
    return correlate(x, gathered, exposure_per_row)


def solution(mesh):
    in_specs = (
        P(("grp", "blk"), None),
        P(("grp", "blk"), None),
        P(("grp", "blk"), None),
        P(("grp", "blk")),
        P(),
        P("grp"),
    )
    out_specs = P("grp", "blk")
    return jax.shard_map(
        functools.partial(shards, mesh.shape["blk"]),
        mesh=mesh,
        in_specs=in_specs,
        out_specs=out_specs,
        check_vma=False,
    )
```
